1024 devices in a mesh: wide: 64 (over x_lo, z), node: 16 (over x_hi, y, core).
Axes of the slice: x: 4 (x_hi: 2, x_lo: 2; x = x_hi * 2 + x_lo), y: 4, z: 32, core: 2. Of those that a mesh axis runs over, the one named last changes fastest.
Arguments:
- tokens: bfloat16 [131072, 12288], P(('wide', 'node')), may hold values from -24 to 24
- weight_codes: bfloat16 [12288, 128], P('wide', 'node'), may hold values from -4 to 4
- block_scales: bfloat16 [96, 128], P(None, 'node'), may hold values from 0.0029907227 to 0.029907227
- cotangent: bfloat16 [131072, 128], P(('wide', 'node')), may hold values from -0.016479492 to 0.016479492
Outputs:
- projected: bfloat16 [131072, 128], P(('wide', 'node'))
- weight_grad: float32 [12288, 128], P('wide', 'node')
The draws below stay inside these ranges and needn't reach their ends.
All inputs are finite; a program needn't handle non-finite values.
Results may differ from the reference program's by a relative error of at most 0.015.
Values may be sent and summed in bfloat16 or wider, within the bound.
A program may use at most 64 MiB of HBM per device.

```python
import math
import jax
import jax.numpy as jnp
from jax import lax

D = 12288
K = 128
BLOCK = 128
TOK_DEV = 128
TOKENS = 131072
N_WIDE = 64
N_NODE = 16


def strengthened(entries, rng, source, target, shards_of, factor):
    def block_of(dim):
        return (jnp.arange(entries.shape[dim]) // (entries.shape[dim] // shards_of)).reshape((-1,) + (1,) * (entries.ndim - 1 - dim))

    first = jax.random.permutation(rng, shards_of)[block_of(target)]
    second = (block_of(target) + shards_of // 2) % shards_of
    return jnp.where((block_of(source) == first) | (block_of(source) == second), factor * entries, entries)


def steps_of(stream_key, extent, shards, low, top_value):
    def one(axis_at, shards_of):
        steps = jax.random.uniform(jax.random.fold_in(jax.random.fold_in(stream_key, 6), axis_at), (shards_of,), jnp.float32, low / len(shards), top_value / len(shards))
        return jnp.repeat(jnp.exp(steps), extent[axis_at] // shards_of).reshape((-1,) + (1,) * (len(extent) - axis_at - 1))

    factor_of = one(*shards[0])
    for cut in shards[1:]:
        factor_of = factor_of * one(*cut)
    return factor_of


def scatter_about(stream_key, shape, width, limit, split=(), kind=jnp.bfloat16):
    result = width * jax.random.normal(stream_key, shape, jnp.float32)
    if split:
        result = result * steps_of(stream_key, shape, split, -0.22, 0.18)
    return jnp.clip(result, -limit, limit).astype(kind)


def bell_draw_with(own_key, shape, deviation, limit, shards, heavy, kind=jnp.bfloat16):
    drawn = deviation * jax.random.normal(own_key, shape, jnp.float32)
    if shards:
        drawn = drawn * steps_of(own_key, shape, shards, -0.22, 0.18)
    return jnp.clip(strengthened(drawn, jax.random.fold_in(own_key, 3), *heavy), -limit, limit).astype(kind)


def setup_inputs(seed: int = 0) -> dict:
    keys = jax.random.split(jax.random.key(seed), 5)
    return {
        "tokens": bell_draw_with(keys[0], (TOKENS, D), 1.0, 24.0, ((0, 1024),), (0, 1, 1024, 6.0)),
        "weight_codes": scatter_about(keys[1], (D, K), 1.0, 4.0, ((0, 64), (1, 16))),
        "block_scales": jnp.clip(jnp.exp(math.log(0.029907227) - 2.3025851 * jax.random.uniform(keys[2], (D // BLOCK, K), jnp.float32) ** steps_of(keys[2], (D // BLOCK, K), ((1, 16),), -0.2, 0.2)), 0.0029907227, 0.029907227).astype(jnp.bfloat16),
        "cotangent": scatter_about(keys[3], (TOKENS, K), (TOKENS ** -0.5), 0.016479492, ((0, 1024),)),
    }


def reference(tokens, weight_codes, block_scales, cotangent):
    factor = jnp.repeat(block_scales.astype(jnp.float32), BLOCK, axis=0)
    weight = (weight_codes.astype(jnp.float32) * factor).astype(jnp.bfloat16)
    projected = jnp.dot(tokens, weight, preferred_element_type=jnp.float32).astype(jnp.bfloat16)
    token_blocks = tokens.reshape(N_WIDE, N_NODE, TOK_DEV, D)
    cot_blocks = cotangent.reshape(N_WIDE, N_NODE, TOK_DEV, K)

    def node_step(acc, pair):
        part = lax.dot_general(pair[0], pair[1], (((0,), (0,)), ((), ())), preferred_element_type=jnp.float32)
        part = lax.optimization_barrier(part.astype(jnp.bfloat16))
        return acc + part.astype(jnp.float32), None

    def wide_step(acc, pair):
        node_sum, unused = lax.scan(node_step, jnp.zeros((D, K), jnp.float32), pair)
        return acc + node_sum, None

    weight_grad, unused = lax.scan(wide_step, jnp.zeros((D, K), jnp.float32), (token_blocks, cot_blocks))
    return projected, weight_grad
```

```python
import jax
import jax.numpy as jnp
from jax import lax
from jax.experimental import pallas as pl
from jax.experimental.pallas import tpu as pltpu
from jax.sharding import PartitionSpec as P

MESH = pl.DeviceIdType.MESH
BF16 = jnp.bfloat16
F32 = jnp.float32
NX = 4
NY = 4
NZ = 32
RES = 8
ROWS = 192
COLS = 16
SPAN = RES * ROWS
PAD = 256
BLOCK = 128


def mod(a, n):
    return lax.rem(a + n, n)


def dot(a, b, ca, cb):
    return lax.dot_general(a, b, (((ca,), (cb,)), ((), ())), preferred_element_type=F32)


def kernel(
    tok_hbm, codes, scales, cot, proj, wg,
    T, C2, cotT, W, G, R1, S1, R2, F0, A, Ar, Zb, Zs, Zr, Zq, Zr2, V, Psum, Pr,
    tl_sem, ts_sem, tr_sem, c_sem, a_sem, v_sem, p_sem,
    z1s_sem, z1r_sem, z2s_sem, z2r_sem,
    r1s_sem, r1r_sem, r2s_sem, r2r_sem,
    a1s_sem, a1r_sem, a2s_sem, a2r_sem,
    q1s_sem, q1r_sem, q2s_sem, q2r_sem,
):
    wide, node = lax.axis_index("wide"), lax.axis_index("node")
    x_lo, z = wide // NZ, lax.rem(wide, NZ)
    x_hi, y, core = node // (2 * NY), lax.rem(node // 2, NY), lax.rem(node, 2)
    x = 2 * x_hi + x_lo
    res, octet = lax.rem(z, RES), z // RES
    odd = lax.rem(z, 2)
    lead = core == z // 16

    def dev(dx=0, dy=0, dz=0, sibling=False):
        xx, yy, zz = lax.rem(x + dx, NX), lax.rem(y + dy, NY), lax.rem(z + dz, NZ)
        cc = 1 - core if sibling else core
        return (lax.rem(xx, 2) * NZ + zz, (xx // 2) * (2 * NY) + yy * 2 + cc)

    def rows(xx, yy):
        return pl.ds(pl.multiple_of(COLS * ((xx // 2) * NY + yy), COLS), COLS)

    def remote(src, dst, send, recv, to):
        return pltpu.make_async_remote_copy(
            src_ref=src, dst_ref=dst, send_sem=send, recv_sem=recv, device_id=to, device_id_type=MESH
        )

    def wait(ref, sem):
        pltpu.make_async_copy(ref, ref, sem).wait()

    near = (1, NZ - 1, 2, NZ - 2, 3, NZ - 3)
    partners = [dev(sibling=True)]
    partners += [dev(dx=k) for k in (1, 2, 3)] + [dev(dy=k) for k in (1, 2, 3)]
    partners += [dev(dz=k) for k in near + (4, NZ - 4)] + [dev(dz=k) for k in (8, 16, 24)]

    barrier = pltpu.get_barrier_semaphore()
    for to in partners:
        pl.semaphore_signal(barrier, inc=1, device_id=to, device_id_type=MESH)

    def columns(xl, half, h):
        return pl.ds(pl.multiple_of(xl * NZ * ROWS + half * 2 * SPAN + h * SPAN, SPAN), SPAN)

    for h in range(2):
        for xl in range(2):
            pltpu.make_async_copy(
                tok_hbm.at[:, columns(xl, core, h)], T.at[xl, h, pl.ds(0, 128)], tl_sem.at[xl, h]
            ).start()

    nb = scales.shape[1]
    block_of = (lax.broadcasted_iota(jnp.int32, (ROWS, nb), 0) + wide * ROWS) // BLOCK
    pick = (block_of == lax.broadcasted_iota(jnp.int32, (ROWS, nb), 1)).astype(BF16)
    factor = dot(scales[...], pick, 1, 1)
    weight = (codes[...].astype(F32) * factor).astype(BF16).astype(F32)
    blank = jnp.zeros((8, PAD - ROWS), F32)
    weight = jnp.where(odd == 1, jnp.concatenate([blank, weight], 1), jnp.concatenate([weight, blank], 1))
    blank = jnp.zeros((8, PAD), F32)
    A[...] = jnp.where(
        core == 0, jnp.concatenate([weight, blank], 0), jnp.concatenate([blank, weight], 0)
    ).astype(BF16)
    eye = (lax.broadcasted_iota(jnp.int32, (128, 128), 0) == lax.broadcasted_iota(jnp.int32, (128, 128), 1)).astype(BF16)

    pl.semaphore_wait(barrier, len(partners))

    sib = dev(sibling=True)
    a_copy = remote(A, Ar, a_sem.at[0], a_sem.at[1], sib)

    @pl.when(jnp.logical_not(lead))
    def _():
        a_copy.start()

    cot_copy = remote(cot, C2, c_sem.at[0], c_sem.at[1], sib)
    cot_copy.start()
    tok_copy = {}
    for h in range(2):
        for xl in range(2):
            tok_copy[xl, h] = remote(
                tok_hbm.at[:, columns(xl, 1 - core, h)],
                T.at[xl, h, pl.ds(128, 128)],
                ts_sem.at[xl, h],
                tr_sem.at[xl, h],
                sib,
            )
            tok_copy[xl, h].start()

    @pl.when(lead)
    def _():
        wait(Ar, a_sem.at[1])
        for h in range(2):

            @pl.when(lax.rem(octet, 2) == h)
            def _():
                Zb[res, h] = A[...] + Ar[...]
                for k in (8, 16, 24):
                    remote(Zb.at[res, h], Zb.at[res, h], z1s_sem, z1r_sem.at[h], dev(dz=k)).start()

    cotT[:, pl.ds(0, 128)] = dot(eye, cot[...], 1, 1).astype(BF16)
    cot_copy.wait_recv()
    cotT[:, pl.ds(128, 128)] = dot(eye, C2[...], 1, 1).astype(BF16)

    def grad(h):
        for xl in range(2):
            wait(T.at[xl, h, pl.ds(0, 128)], tl_sem.at[xl, h])
            tok_copy[xl, h].wait_recv()

            def tile(i, carry):
                at = pl.ds(pl.multiple_of(i * 512, 512), 512)
                G[xl, h, :, at] = dot(cotT[...], T[xl, h, :, at], 1, 0).astype(BF16)
                return carry

            lax.fori_loop(0, SPAN // 512, tile, 0)

    def piece(j, k, h):
        return (lax.rem(x + j, NX), lax.rem(y + k, NY)) if h == 0 else (lax.rem(x + k, NX), lax.rem(y + j, NY))

    def over(k, h):
        return dev(dy=k) if h == 0 else dev(dx=k)

    def send_grad(h):
        for j in (1, 2, 3, 0):
            for k in (1, 3, 2):
                xx, yy = piece(j, k, h)
                remote(
                    G.at[lax.rem(xx, 2), h, rows(xx, yy)], R1.at[h, k - 1, j], r1s_sem, r1r_sem.at[h, k - 1, j], over(k, h)
                ).start()

    grad(0)
    send_grad(0)

    for h in range(2):

        @pl.when(octet != 2 * core + h)
        def _():
            wait(Zb.at[res, h], z1r_sem.at[h])

    for i, k in enumerate(near):
        remote(Zb.at[res], Zb.at[res], z2s_sem, z2r_sem.at[i], dev(dz=k)).start()
    for h, k in ((0, 4), (1, NZ - 4)):
        remote(Zb.at[res, h], Zb.at[res, h], z2s_sem, z2r_sem.at[6 + h], dev(dz=k)).start()

    grad(1)
    send_grad(1)

    for i, k in enumerate(near):
        wait(Zb.at[lax.rem(res + 2 * RES - (k if k < RES else k - NZ), RES)], z2r_sem.at[i])
    for h in range(2):
        wait(Zb.at[lax.rem(res + 4, RES), h], z2r_sem.at[6 + h])
    mine = rows(x, y)
    for h in range(2):
        for j in range(RES // 2):
            at = 384 * j
            W[x_lo, h, mine, at : at + 128] = Zb[2 * j, h, :, 0:128]
            W[x_lo, h, mine, at + 128 : at + 256] = Zb[2 * j, h, :, 128:256] + Zb[2 * j + 1, h, :, 0:128]
            W[x_lo, h, mine, at + 256 : at + 384] = Zb[2 * j + 1, h, :, 128:256]

    for k in (1, 3, 2):
        for h in range(2):
            here = W.at[x_lo, h, mine]
            remote(here, here, a1s_sem, a1r_sem.at[h, k - 1], over(k, 1 - h)).start()

    for h in range(2):
        for j in (1, 2, 3, 0):
            xx, yy = piece(j, 0, h)
            total = G[lax.rem(xx, 2), h, rows(xx, yy)].astype(F32)
            for k in (1, 3, 2):
                wait(R1.at[h, k - 1, j], r1r_sem.at[h, k - 1, j])
                total += R1[h, k - 1, j].astype(F32)
            if j == 0:
                F0[h] = total
            else:
                S1[h, j - 1] = total.astype(BF16)
                remote(S1.at[h, j - 1], R2.at[h, j - 1], r2s_sem, r2r_sem.at[h, j - 1], over(j, 1 - h)).start()

    def origin(j, k, h):
        return (mod(x - j, NX), mod(y - k, NY)) if h == 0 else (mod(x - k, NX), mod(y - j, NY))

    def part(j, k, h):
        xx, yy = origin(j, k, h)
        return W.at[lax.rem(xx, 2), h, rows(xx, yy)]

    for j in (0, 1, 3, 2):
        for h in range(2):
            here = part(j, 0, h)
            if j:
                wait(here, a1r_sem.at[h, j - 1])
            for k in (1, 3, 2):
                remote(here, here, a2s_sem, a2r_sem.at[h, k - 1, j], over(k, h)).start()

    for h in range(2):
        total = F0[h]
        for j in (1, 3, 2):
            wait(R2.at[h, j - 1], r2r_sem.at[h, j - 1])
            total += R2[h, j - 1].astype(F32)
        total = total.astype(BF16)
        for j in range(RES // 2):
            Zs[2 * j, h] = total[:, 384 * j : 384 * j + 256]
            Zs[2 * j + 1, h] = total[:, 384 * j + 128 : 384 * j + 384]

    for i, k in enumerate(near):
        remote(Zs.at[lax.rem(res + k, RES)], Zr.at[i], q1s_sem, q1r_sem.at[i], dev(dz=k)).start()
    for h, k in ((0, 4), (1, NZ - 4)):
        remote(Zs.at[lax.rem(res + 4, RES), h], Zr.at[6, h], q1s_sem, q1r_sem.at[6 + h], dev(dz=k)).start()
    for i in range(6):
        wait(Zr.at[i], q1r_sem.at[i])
    for h in range(2):
        wait(Zr.at[6, h], q1r_sem.at[6 + h])
    total = Zs[res].astype(F32)
    for i in range(7):
        total += Zr[i].astype(F32)
    Zq[...] = total.astype(BF16)

    for h in range(2):
        hop = lax.rem(2 * core + h - octet + 4, 4)
        for k in (1, 2, 3):

            @pl.when(hop == k)
            def _():
                remote(Zq.at[h], Zr2.at[k - 1], q2s_sem.at[h], q2r_sem.at[k - 1], dev(dz=8 * k)).start()

    v_copy = remote(V, V, v_sem.at[0], v_sem.at[1], sib)

    @pl.when(lead)
    def _():
        total = Zq[lax.rem(octet, 2)].astype(F32)
        for k in (1, 2, 3):
            wait(Zr2.at[k - 1], q2r_sem.at[k - 1])
            total += Zr2[k - 1].astype(F32)
        V[...] = total
        v_copy.start()

    acc = None
    for h in range(2):
        for k in (1, 3, 2):
            for j in range(4):
                wait(part(j, k, h), a2r_sem.at[h, k - 1, j])
        for xl in range(2):
            term = dot(T[xl, h], W[xl, h], 1, 1)
            acc = term if acc is None else acc + term
    Psum[...] = acc
    p_copy = remote(Psum.at[pl.ds(128, 128)], Pr, p_sem.at[0], p_sem.at[1], sib)
    p_copy.start()

    @pl.when(jnp.logical_not(lead))
    def _():
        v_copy.wait_recv()

    picked = jnp.where(core == 0, V[0:8], V[8:16])
    picked = jnp.where(odd == 1, picked[:, 64:PAD], picked[:, 0:ROWS])
    wg[...] = picked

    p_copy.wait_recv()
    proj[...] = (Psum[0:128] + Pr[...]).astype(BF16)

    p_copy.wait_send()
    cot_copy.wait_send()
    for copy in tok_copy.values():
        copy.wait_send()

    @pl.when(lead)
    def _():
        v_copy.wait_send()
        wait(Zr2, z1s_sem)

    @pl.when(jnp.logical_not(lead))
    def _():
        a_copy.wait_send()

    wait(Zr, z2s_sem)
    wait(Zr, q1s_sem)
    wait(R1, r1s_sem)
    wait(R1, a2s_sem)
    wait(R2, r2s_sem)
    wait(R2, a1s_sem)
    for h in range(2):

        @pl.when(octet != 2 * core + h)
        def _():
            wait(Zq.at[h], q2s_sem.at[h])


def on_device(tokens, weight_codes, block_scales, cotangent):
    vmem = pl.BlockSpec(memory_space=pltpu.VMEM)
    dma = pltpu.SemaphoreType.DMA
    projected, turned = pl.pallas_call(
        kernel,
        out_shape=(
            jax.ShapeDtypeStruct((128, 128), BF16),
            jax.ShapeDtypeStruct((8, ROWS), F32),
        ),
        in_specs=[pl.BlockSpec(memory_space=pl.ANY), vmem, vmem, vmem],
        out_specs=(vmem, vmem),
        scratch_shapes=[
            pltpu.VMEM((2, 2, 256, SPAN), BF16),
            pltpu.VMEM((128, 128), BF16),
            pltpu.VMEM((128, 256), BF16),
            pltpu.VMEM((2, 2, 128, SPAN), BF16),
            pltpu.VMEM((2, 2, 128, SPAN), BF16),
            pltpu.VMEM((2, 3, 4, COLS, SPAN), BF16),
            pltpu.VMEM((2, 3, COLS, SPAN), BF16),
            pltpu.VMEM((2, 3, COLS, SPAN), BF16),
            pltpu.VMEM((2, COLS, SPAN), F32),
            pltpu.VMEM((COLS, PAD), BF16),
            pltpu.VMEM((COLS, PAD), BF16),
            pltpu.VMEM((RES, 2, COLS, PAD), BF16),
            pltpu.VMEM((RES, 2, COLS, PAD), BF16),
            pltpu.VMEM((7, 2, COLS, PAD), BF16),
            pltpu.VMEM((2, COLS, PAD), BF16),
            pltpu.VMEM((3, COLS, PAD), BF16),
            pltpu.VMEM((COLS, PAD), F32),
            pltpu.VMEM((256, 128), F32),
            pltpu.VMEM((128, 128), F32),
            dma((2, 2)),
            dma((2, 2)),
            dma((2, 2)),
            dma((2,)),
            dma((2,)),
            dma((2,)),
            dma((2,)),
            dma,
            dma((2,)),
            dma,
            dma((8,)),
            dma,
            dma((2, 3, 4)),
            dma,
            dma((2, 3)),
            dma,
            dma((2, 3)),
            dma,
            dma((2, 3, 4)),
            dma,
            dma((8,)),
            dma((2,)),
            dma((3,)),
        ],
        compiler_params=pltpu.CompilerParams(
            collective_id=0, has_side_effects=True, vmem_limit_bytes=60 * 1024 * 1024
        ),
    )(tokens, weight_codes.T, block_scales.T, cotangent)
    return projected, turned.T


def solution(mesh):
    placed = (
        P(("wide", "node"), None),
        P("wide", "node"),
        P(None, "node"),
        P(("wide", "node"), None),
    )
    return jax.shard_map(
        on_device,
        mesh=mesh,
        in_specs=placed,
        out_specs=(P(("wide", "node"), None), P("wide", "node")),
        check_vma=False,
    )
```

```python
import jax
import jax.numpy as jnp
from jax import lax
from jax.experimental import pallas as pl
from jax.experimental.pallas import tpu as pltpu
from jax.sharding import PartitionSpec as P

MESH = pl.DeviceIdType.MESH
BF16 = jnp.bfloat16
F32 = jnp.float32
NX = 4
NY = 4
NZ = 32
RES = 8
ROWS = 192
COLS = 16
SPAN = RES * ROWS
PAD = 256
BLOCK = 128


def mod(a, n):
    return lax.rem(a + n, n)


def dot(a, b, ca, cb):
    return lax.dot_general(a, b, (((ca,), (cb,)), ((), ())), preferred_element_type=F32)


def kernel(
    tok_hbm, codes, scales, cot, proj, wg,
    T, C2, cotT, W, G, R1, S1, R2, F0, A, Ar, Zb, Zs, Zr, Zq, Zr2, Psum, Pr,
    tl_sem, ts_sem, tr_sem, c_sem, a_sem, v_sem, p_sem,
    n_sem, z1s_sem, z1r_sem, z2s_sem, z2r_sem,
    r1s_sem, r1r_sem, r2s_sem, r2r_sem,
    a1s_sem, a1r_sem, a2s_sem, a2r_sem,
    q1s_sem, q1r_sem, q2s_sem, q2r_sem,
):
    wide, node = lax.axis_index("wide"), lax.axis_index("node")
    x_lo, z = wide // NZ, lax.rem(wide, NZ)
    x_hi, y, core = node // (2 * NY), lax.rem(node // 2, NY), lax.rem(node, 2)
    x = 2 * x_hi + x_lo
    res, octet = lax.rem(z, RES), z // RES
    odd = lax.rem(z, 2)
    lead = core == z // 16

    def dev(dx=0, dy=0, dz=0, sibling=False):
        xx, yy, zz = lax.rem(x + dx, NX), lax.rem(y + dy, NY), lax.rem(z + dz, NZ)
        cc = 1 - core if sibling else core
        return (lax.rem(xx, 2) * NZ + zz, (xx // 2) * (2 * NY) + yy * 2 + cc)

    def rows(xx, yy):
        return pl.ds(pl.multiple_of(COLS * ((xx // 2) * NY + yy), COLS), COLS)

    def remote(src, dst, send, recv, to):
        return pltpu.make_async_remote_copy(
            src_ref=src, dst_ref=dst, send_sem=send, recv_sem=recv, device_id=to, device_id_type=MESH
        )

    def wait(ref, sem):
        pltpu.make_async_copy(ref, ref, sem).wait()

    near = (3, NZ - 3, 2, NZ - 2, 1, NZ - 1)
    partners = [dev(sibling=True)]
    partners += [dev(dx=k) for k in (1, 2, 3)] + [dev(dy=k) for k in (1, 2, 3)]
    partners += [dev(dz=k) for k in near + (4, NZ - 4)]

    barrier = pltpu.get_barrier_semaphore()
    for to in partners:
        pl.semaphore_signal(barrier, inc=1, device_id=to, device_id_type=MESH)

    def columns(xl, half, h):
        return pl.ds(pl.multiple_of(xl * NZ * ROWS + half * 2 * SPAN + h * SPAN, SPAN), SPAN)

    chunks = [(lax.rem(x_lo + 1 + a, 2), a, h) for a in range(2) for h in range(2)]
    for xl, a, h in chunks:
        pltpu.make_async_copy(
            tok_hbm.at[:, columns(xl, core, h)], T.at[xl, h, pl.ds(0, 128)], tl_sem.at[a, h]
        ).start()

    nb = scales.shape[1]
    block_of = (lax.broadcasted_iota(jnp.int32, (ROWS, nb), 0) + wide * ROWS) // BLOCK
    pick = (block_of == lax.broadcasted_iota(jnp.int32, (ROWS, nb), 1)).astype(BF16)
    factor = dot(scales[...], pick, 1, 1)
    weight = (codes[...].astype(F32) * factor).astype(BF16).astype(F32)
    blank = jnp.zeros((8, PAD - ROWS), F32)
    weight = jnp.where(odd == 1, jnp.concatenate([blank, weight], 1), jnp.concatenate([weight, blank], 1))
    blank = jnp.zeros((8, PAD), F32)
    A[...] = jnp.where(
        core == 0, jnp.concatenate([weight, blank], 0), jnp.concatenate([blank, weight], 0)
    ).astype(BF16)
    eye = (lax.broadcasted_iota(jnp.int32, (128, 128), 0) == lax.broadcasted_iota(jnp.int32, (128, 128), 1)).astype(BF16)

    pl.semaphore_wait(barrier, len(partners))
    for k in (4, NZ - 4):
        pl.semaphore_signal(n_sem, inc=1, device_id=dev(dz=k), device_id_type=MESH)

    sib = dev(sibling=True)
    a_copy = remote(A, Ar, a_sem.at[0], a_sem.at[1], sib)

    @pl.when(jnp.logical_not(lead))
    def _():
        a_copy.start()

    cot_copy = remote(cot, C2, c_sem.at[0], c_sem.at[1], sib)
    cot_copy.start()
    tok_copy = {}
    for xl, a, h in chunks:
        tok_copy[a, h] = remote(
            tok_hbm.at[:, columns(xl, 1 - core, h)],
            T.at[xl, h, pl.ds(128, 128)],
            ts_sem.at[a, h],
            tr_sem.at[a, h],
            sib,
        )
        tok_copy[a, h].start()

    pl.semaphore_wait(n_sem, 2)

    def onward(h, i, k):
        here = Zb.at[res, h]
        return remote(here, here, z1s_sem.at[h, i], z1r_sem.at[h], dev(dz=k))

    place = [lax.rem(octet - 2 * core - h + 4, 4) for h in range(2)]

    @pl.when(lead)
    def _():
        wait(Ar, a_sem.at[1])
        for h in range(2):

            @pl.when(place[h] == 0)
            def _():
                Zb[res, h] = A[...] + Ar[...]
                onward(h, 0, 8).start()
                onward(h, 1, 24).start()

    cotT[:, pl.ds(0, 128)] = dot(eye, cot[...], 1, 1).astype(BF16)
    cot_copy.wait_recv()
    cotT[:, pl.ds(128, 128)] = dot(eye, C2[...], 1, 1).astype(BF16)

    def grad(xl, a, h):
        wait(T.at[xl, h, pl.ds(0, 128)], tl_sem.at[a, h])
        tok_copy[a, h].wait_recv()

        def tile(i, carry):
            at = pl.ds(pl.multiple_of(i * 512, 512), 512)
            G[xl, h, :, at] = dot(cotT[...], T[xl, h, :, at], 1, 0).astype(BF16)
            return carry

        lax.fori_loop(0, SPAN // 512, tile, 0)

    def piece(j, k, h):
        return (lax.rem(x + j, NX), lax.rem(y + k, NY)) if h == 0 else (lax.rem(x + k, NX), lax.rem(y + j, NY))

    def over(k, h):
        return dev(dy=k) if h == 0 else dev(dx=k)

    def send_grad(a, h):
        if h == 0:
            pairs = [(j, k) for j in ((1, 3), (2, 0))[a] for k in (2, 1, 3)]
        else:
            pairs = [(j, k) for j in (1, 3, 2, 0) for k in ((1, 3), (2,))[a]]
        for j, k in pairs:
            xx, yy = piece(j, k, h)
            remote(
                G.at[lax.rem(xx, 2), h, rows(xx, yy)], R1.at[h, k - 1, j], r1s_sem, r1r_sem.at[h, k - 1, j], over(k, h)
            ).start()

    for xl, a, h in chunks:
        grad(xl, a, h)
        send_grad(a, h)

    for h in range(2):

        @pl.when(place[h] == 1)
        def _():
            wait(Zb.at[res, h], z1r_sem.at[h])
            onward(h, 0, 8).start()

    for h in range(2):

        @pl.when(place[h] >= 2)
        def _():
            wait(Zb.at[res, h], z1r_sem.at[h])

    for h, k in ((0, 4), (1, NZ - 4)):
        remote(Zb.at[res, h], Zb.at[res, h], z2s_sem, z2r_sem.at[6 + h], dev(dz=k)).start()
    for i, k in enumerate(near):
        remote(Zb.at[res], Zb.at[res], z2s_sem, z2r_sem.at[i], dev(dz=k)).start()

    for h in range(2):
        for j in (1, 3, 2, 0):
            xx, yy = piece(j, 0, h)
            total = G[lax.rem(xx, 2), h, rows(xx, yy)].astype(F32)
            for k in (1, 3, 2):
                wait(R1.at[h, k - 1, j], r1r_sem.at[h, k - 1, j])
                total += R1[h, k - 1, j].astype(F32)
            if j == 0:
                F0[h] = total
            else:
                S1[h, j - 1] = total.astype(BF16)
                remote(S1.at[h, j - 1], R2.at[h, j - 1], r2s_sem, r2r_sem.at[h, j - 1], over(j, 1 - h)).start()

    for i, k in enumerate(near):
        wait(Zb.at[lax.rem(res + 2 * RES - (k if k < RES else k - NZ), RES)], z2r_sem.at[i])
    for h in range(2):
        wait(Zb.at[lax.rem(res + 4, RES), h], z2r_sem.at[6 + h])
    mine = rows(x, y)
    for h in range(2):
        for j in range(RES // 2):
            at = 384 * j
            W[x_lo, h, mine, at : at + 128] = Zb[2 * j, h, :, 0:128]
            W[x_lo, h, mine, at + 128 : at + 256] = Zb[2 * j, h, :, 128:256] + Zb[2 * j + 1, h, :, 0:128]
            W[x_lo, h, mine, at + 256 : at + 384] = Zb[2 * j + 1, h, :, 128:256]

    for k in (1, 3, 2):
        for h in range(2):
            here = W.at[x_lo, h, mine]
            remote(here, here, a1s_sem, a1r_sem.at[h, k - 1], over(k, 1 - h)).start()

    for h in range(2):
        total = F0[h]
        for j in (1, 3, 2):
            wait(R2.at[h, j - 1], r2r_sem.at[h, j - 1])
            total += R2[h, j - 1].astype(F32)
        total = total.astype(BF16)
        for j in range(RES // 2):
            Zs[2 * j, h] = total[:, 384 * j : 384 * j + 256]
            Zs[2 * j + 1, h] = total[:, 384 * j + 128 : 384 * j + 384]

    for h, k in ((0, 4), (1, NZ - 4)):
        remote(Zs.at[lax.rem(res + 4, RES), h], Zr.at[6, h], q1s_sem, q1r_sem.at[6 + h], dev(dz=k)).start()
    for i, k in enumerate(near):
        remote(Zs.at[lax.rem(res + k, RES)], Zr.at[i], q1s_sem, q1r_sem.at[i], dev(dz=k)).start()
    def origin(j, k, h):
        return (mod(x - j, NX), mod(y - k, NY)) if h == 0 else (mod(x - k, NX), mod(y - j, NY))

    def part(j, k, h):
        xx, yy = origin(j, k, h)
        return W.at[lax.rem(xx, 2), h, rows(xx, yy)]

    for j in (0, 1, 3, 2):
        for h in range(2):
            here = part(j, 0, h)
            if j:
                wait(here, a1r_sem.at[h, j - 1])
            for k in (1, 3, 2):
                remote(here, here, a2s_sem, a2r_sem.at[h, k - 1, j], over(k, h)).start()

    for i in range(6):
        wait(Zr.at[i], q1r_sem.at[i])
    for h in range(2):
        wait(Zr.at[6, h], q1r_sem.at[6 + h])
    total = Zs[res].astype(F32)
    for i in range(7):
        total += Zr[i].astype(F32)
    Zq[...] = total.astype(BF16)

    def out_of(h, k, both):
        return remote(
            Zq.at[h], Zr2.at[k - 1], q2s_sem.at[h, both], q2r_sem.at[k - 1], dev(dz=8 * k, sibling=both == 1)
        )

    for h in range(2):
        for k in (2, 1, 3):

            @pl.when(place[h] == 4 - k)
            def _():
                out_of(h, k, 0).start()
                out_of(h, k, 1).start()

    own = Zq.at[lax.rem(octet, 2)]
    v_copy = remote(own, Zr2.at[3], v_sem.at[0], v_sem.at[1], sib)

    @pl.when(lead)
    def _():
        v_copy.start()
        Zr2[3] = own[...]

    acc = None
    for h in range(2):
        for k in (1, 3, 2):
            for j in range(4):
                wait(part(j, k, h), a2r_sem.at[h, k - 1, j])
        for xl in range(2):
            term = dot(T[xl, h], W[xl, h], 1, 1)
            acc = term if acc is None else acc + term
    Psum[...] = acc
    p_copy = remote(Psum.at[pl.ds(128, 128)], Pr, p_sem.at[0], p_sem.at[1], sib)
    p_copy.start()

    @pl.when(jnp.logical_not(lead))
    def _():
        v_copy.wait_recv()

    total = Zr2[3].astype(F32)
    for k in (1, 2, 3):
        wait(Zr2.at[k - 1], q2r_sem.at[k - 1])
        total += Zr2[k - 1].astype(F32)
    picked = jnp.where(core == 0, total[0:8], total[8:16])
    wg[...] = jnp.where(odd == 1, picked[:, 64:PAD], picked[:, 0:ROWS])

    p_copy.wait_recv()
    proj[...] = (Psum[0:128] + Pr[...]).astype(BF16)

    p_copy.wait_send()
    cot_copy.wait_send()
    for copy in tok_copy.values():
        copy.wait_send()

    @pl.when(lead)
    def _():
        v_copy.wait_send()

    @pl.when(jnp.logical_not(lead))
    def _():
        a_copy.wait_send()

    wait(Zr, z2s_sem)
    wait(Zr, q1s_sem)
    wait(R1, r1s_sem)
    wait(R1, a2s_sem)
    wait(R2, r2s_sem)
    wait(R2, a1s_sem)
    for h in range(2):

        @pl.when(place[h] != 0)
        def _():
            wait(Zq.at[h], q2s_sem.at[h, 0])
            wait(Zq.at[h], q2s_sem.at[h, 1])

        @pl.when(place[h] == 0)
        def _():
            wait(Zb.at[res, h], z1s_sem.at[h, 1])

        @pl.when(place[h] <= 1)
        def _():
            wait(Zb.at[res, h], z1s_sem.at[h, 0])


def on_device(tokens, weight_codes, block_scales, cotangent):
    vmem = pl.BlockSpec(memory_space=pltpu.VMEM)
    dma = pltpu.SemaphoreType.DMA
    projected, turned = pl.pallas_call(
        kernel,
        out_shape=(
            jax.ShapeDtypeStruct((128, 128), BF16),
            jax.ShapeDtypeStruct((8, ROWS), F32),
        ),
        in_specs=[pl.BlockSpec(memory_space=pltpu.HBM), vmem, vmem, vmem],
        out_specs=(vmem, vmem),
        scratch_shapes=[
            pltpu.VMEM((2, 2, 256, SPAN), BF16),
            pltpu.VMEM((128, 128), BF16),
            pltpu.VMEM((128, 256), BF16),
            pltpu.VMEM((2, 2, 128, SPAN), BF16),
            pltpu.VMEM((2, 2, 128, SPAN), BF16),
            pltpu.VMEM((2, 3, 4, COLS, SPAN), BF16),
            pltpu.VMEM((2, 3, COLS, SPAN), BF16),
            pltpu.VMEM((2, 3, COLS, SPAN), BF16),
            pltpu.VMEM((2, COLS, SPAN), F32),
            pltpu.VMEM((COLS, PAD), BF16),
            pltpu.VMEM((COLS, PAD), BF16),
            pltpu.VMEM((RES, 2, COLS, PAD), BF16),
            pltpu.VMEM((RES, 2, COLS, PAD), BF16),
            pltpu.VMEM((7, 2, COLS, PAD), BF16),
            pltpu.VMEM((2, COLS, PAD), BF16),
            pltpu.VMEM((4, COLS, PAD), BF16),
            pltpu.VMEM((256, 128), F32),
            pltpu.VMEM((128, 128), F32),
            dma((2, 2)),
            dma((2, 2)),
            dma((2, 2)),
            dma((2,)),
            dma((2,)),
            dma((2,)),
            dma((2,)),
            pltpu.SemaphoreType.REGULAR,
            dma((2, 2)),
            dma((2,)),
            dma,
            dma((8,)),
            dma,
            dma((2, 3, 4)),
            dma,
            dma((2, 3)),
            dma,
            dma((2, 3)),
            dma,
            dma((2, 3, 4)),
            dma,
            dma((8,)),
            dma((2, 2)),
            dma((3,)),
        ],
        compiler_params=pltpu.CompilerParams(
            collective_id=0, has_side_effects=True, vmem_limit_bytes=52 * 1024 * 1024
        ),
    )(tokens, weight_codes.T, block_scales.T, cotangent)
    return projected, turned.T


def solution(mesh):
    placed = (
        P(("wide", "node"), None),
        P("wide", "node"),
        P(None, "node"),
        P(("wide", "node"), None),
    )
    return jax.shard_map(
        on_device,
        mesh=mesh,
        in_specs=placed,
        out_specs=(P(("wide", "node"), None), P("wide", "node")),
        check_vma=False,
    )
```

```python
import jax
import jax.numpy as jnp
from jax import lax
from jax.experimental import pallas as pl
from jax.experimental.pallas import tpu as pltpu
from jax.sharding import PartitionSpec as P

MESH = pl.DeviceIdType.MESH
BF16 = jnp.bfloat16
F32 = jnp.float32
NX = 4
NY = 4
NZ = 32
RES = 8
ROWS = 192
COLS = 16
SPAN = RES * ROWS
PAD = 256
BLOCK = 128


def mod(a, n):
    return lax.rem(a + n, n)


def dot(a, b, ca, cb):
    return lax.dot_general(a, b, (((ca,), (cb,)), ((), ())), preferred_element_type=F32)


def kernel(
    tok_hbm, codes_hbm, scales_hbm, cot_hbm, proj, wg,
    codes, scales, cot,
    T, C2, cotT, W, G, R1, S1, R2, F0, A, Ar, Zb, Zs, Zr, Zq, Zr2, Psum, Pr,
    in_sem, tl_sem, ts_sem, tr_sem, c_sem, a_sem, v_sem, p_sem,
    n_sem, z1s_sem, z1r_sem, z2s_sem, z2r_sem,
    r1s_sem, r1r_sem, r2s_sem, r2r_sem,
    a1s_sem, a1r_sem, a2s_sem, a2r_sem,
    q1s_sem, q1r_sem, q2s_sem, q2r_sem,
):
    wide, node = lax.axis_index("wide"), lax.axis_index("node")
    x_lo, z = wide // NZ, lax.rem(wide, NZ)
    x_hi, y, core = node // (2 * NY), lax.rem(node // 2, NY), lax.rem(node, 2)
    x = 2 * x_hi + x_lo
    res, octet = lax.rem(z, RES), z // RES
    odd = lax.rem(z, 2)
    lead = core == z // 16

    def dev(dx=0, dy=0, dz=0, sibling=False):
        xx, yy, zz = lax.rem(x + dx, NX), lax.rem(y + dy, NY), lax.rem(z + dz, NZ)
        cc = 1 - core if sibling else core
        return (lax.rem(xx, 2) * NZ + zz, (xx // 2) * (2 * NY) + yy * 2 + cc)

    def rows(xx, yy):
        return pl.ds(pl.multiple_of(COLS * ((xx // 2) * NY + yy), COLS), COLS)

    def remote(src, dst, send, recv, to):
        return pltpu.make_async_remote_copy(
            src_ref=src, dst_ref=dst, send_sem=send, recv_sem=recv, device_id=to, device_id_type=MESH
        )

    def wait(ref, sem):
        pltpu.make_async_copy(ref, ref, sem).wait()

    near = (3, NZ - 3, 2, NZ - 2, 1, NZ - 1)
    partners = [dev(sibling=True)]
    partners += [dev(dx=k) for k in (1, 2, 3)] + [dev(dy=k) for k in (1, 2, 3)]
    partners += [dev(dz=k) for k in near + (4, NZ - 4)]

    barrier = pltpu.get_barrier_semaphore()
    for to in partners:
        pl.semaphore_signal(barrier, inc=1, device_id=to, device_id_type=MESH)

    loads = [
        pltpu.make_async_copy(src, dst, in_sem.at[i])
        for i, (src, dst) in enumerate(((codes_hbm, codes), (scales_hbm, scales), (cot_hbm, cot)))
    ]
    for load in loads:
        load.start()

    def columns(xl, half, h):
        return pl.ds(pl.multiple_of(xl * NZ * ROWS + half * 2 * SPAN + h * SPAN, SPAN), SPAN)

    chunks = [(lax.rem(x_lo + 1 + a, 2), a, h) for a in range(2) for h in range(2)]
    for xl, a, h in chunks:
        pltpu.make_async_copy(
            tok_hbm.at[:, columns(xl, core, h)], T.at[xl, h, pl.ds(0, 128)], tl_sem.at[a, h]
        ).start()

    loads[0].wait()
    loads[1].wait()
    nb = scales.shape[1]
    block_of = (lax.broadcasted_iota(jnp.int32, (ROWS, nb), 0) + wide * ROWS) // BLOCK
    pick = (block_of == lax.broadcasted_iota(jnp.int32, (ROWS, nb), 1)).astype(BF16)
    factor = dot(scales[...], pick, 1, 1)
    weight = (codes[...].astype(F32) * factor).astype(BF16).astype(F32)
    blank = jnp.zeros((8, PAD - ROWS), F32)
    weight = jnp.where(odd == 1, jnp.concatenate([blank, weight], 1), jnp.concatenate([weight, blank], 1))
    blank = jnp.zeros((8, PAD), F32)
    A[...] = jnp.where(
        core == 0, jnp.concatenate([weight, blank], 0), jnp.concatenate([blank, weight], 0)
    ).astype(BF16)
    eye = (lax.broadcasted_iota(jnp.int32, (128, 128), 0) == lax.broadcasted_iota(jnp.int32, (128, 128), 1)).astype(BF16)

    pl.semaphore_wait(barrier, len(partners))
    for k in (4, NZ - 4):
        pl.semaphore_signal(n_sem, inc=1, device_id=dev(dz=k), device_id_type=MESH)

    sib = dev(sibling=True)
    a_copy = remote(A, Ar, a_sem.at[0], a_sem.at[1], sib)

    @pl.when(jnp.logical_not(lead))
    def _():
        a_copy.start()

    cot_copy = remote(cot_hbm, C2, c_sem.at[0], c_sem.at[1], sib)
    cot_copy.start()
    tok_copy = {}
    for xl, a, h in chunks:
        tok_copy[a, h] = remote(
            tok_hbm.at[:, columns(xl, 1 - core, h)],
            T.at[xl, h, pl.ds(128, 128)],
            ts_sem.at[a, h],
            tr_sem.at[a, h],
            sib,
        )
        tok_copy[a, h].start()

    loads[2].wait()
    cotT[:, pl.ds(0, 128)] = dot(eye, cot[...], 1, 1).astype(BF16)
    cot_copy.wait_recv()
    cotT[:, pl.ds(128, 128)] = dot(eye, C2[...], 1, 1).astype(BF16)

    def grad(xl, a, h):
        wait(T.at[xl, h, pl.ds(0, 128)], tl_sem.at[a, h])
        tok_copy[a, h].wait_recv()

        def tile(i, carry):
            at = pl.ds(pl.multiple_of(i * 512, 512), 512)
            G[xl, h, :, at] = dot(cotT[...], T[xl, h, :, at], 1, 0).astype(BF16)
            return carry

        lax.fori_loop(0, SPAN // 512, tile, 0)

    def piece(j, k, h):
        return (lax.rem(x + j, NX), lax.rem(y + k, NY)) if h == 0 else (lax.rem(x + k, NX), lax.rem(y + j, NY))

    def over(k, h):
        return dev(dy=k) if h == 0 else dev(dx=k)

    def send_grad(a, h):
        if h == 0:
            pairs = [(j, k) for j in ((1, 3), (2, 0))[a] for k in (2, 1, 3)]
        else:
            pairs = [(0, k) for k in ((1, 3), (2,))[a]]
        for j, k in pairs:
            xx, yy = piece(j, k, h)
            if h == 0:
                here, there = rows(xx, yy), pl.ds(COLS * j, COLS)
            else:
                here, there = pl.ds(pl.multiple_of(NY * COLS * (xx // 2), NY * COLS), NY * COLS), pl.ds(0, NY * COLS)
            remote(
                G.at[lax.rem(xx, 2), h, here], R1.at[h, k - 1, there], r1s_sem, r1r_sem.at[h, k - 1, j], over(k, h)
            ).start()

    grad(*chunks[0])
    send_grad(*chunks[0][1:])

    pl.semaphore_wait(n_sem, 2)

    def onward(h, i, k):
        here = Zb.at[res, h]
        return remote(here, here, z1s_sem.at[h, i], z1r_sem.at[h], dev(dz=k))

    place = [lax.rem(octet - 2 * core - h + 4, 4) for h in range(2)]

    @pl.when(lead)
    def _():
        wait(Ar, a_sem.at[1])
        for h in range(2):

            @pl.when(place[h] == 0)
            def _():
                Zb[res, h] = A[...] + Ar[...]
                onward(h, 0, 8).start()
                onward(h, 1, 24).start()

    for xl, a, h in chunks[1:]:
        grad(xl, a, h)
        send_grad(a, h)

    for h in range(2):

        @pl.when(place[h] == 1)
        def _():
            wait(Zb.at[res, h], z1r_sem.at[h])
            onward(h, 0, 8).start()

    first = jnp.where((place[0] == 0) | (place[0] == 3), 0, 1)

    def place_of(h):
        return jnp.where(h == 0, place[0], place[1])

    def spread(h):
        here = Zb.at[res, h]
        remote(here, here, z2s_sem, z2r_sem.at[6, h], dev(dz=jnp.where(h == 0, 4, NZ - 4))).start()
        for i, k in enumerate(near):
            remote(here, here, z2s_sem, z2r_sem.at[i, h], dev(dz=k)).start()

    @pl.when(place_of(first) == 3)
    def _():
        wait(Zb.at[res, first], z1r_sem.at[first])

    spread(first)

    @pl.when(place_of(1 - first) >= 2)
    def _():
        wait(Zb.at[res, 1 - first], z1r_sem.at[1 - first])

    spread(1 - first)

    for h in range(2):
        for j in (1, 3, 2, 0):
            xx, yy = piece(j, 0, h)
            total = G[lax.rem(xx, 2), h, rows(xx, yy)].astype(F32)
            there = pl.ds(COLS * j if h == 0 else pl.multiple_of(COLS * yy, COLS), COLS)
            for k in (1, 3, 2):
                if h == 0:
                    wait(R1.at[h, k - 1, there], r1r_sem.at[h, k - 1, j])
                elif j == 1:
                    wait(R1.at[h, k - 1], r1r_sem.at[h, k - 1, 0])
                total += R1[h, k - 1, there].astype(F32)
            if j == 0:
                F0[h] = total
            else:
                S1[h, j - 1] = total.astype(BF16)
                remote(S1.at[h, j - 1], R2.at[h, j - 1], r2s_sem, r2r_sem.at[h, j - 1], over(j, 1 - h)).start()

    for h in range(2):
        total = F0[h]
        for j in (1, 3, 2):
            wait(R2.at[h, j - 1], r2r_sem.at[h, j - 1])
            total += R2[h, j - 1].astype(F32)
        total = total.astype(BF16)
        for j in range(RES // 2):
            Zs[2 * j, h] = total[:, 384 * j : 384 * j + 256]
            Zs[2 * j + 1, h] = total[:, 384 * j + 128 : 384 * j + 384]

    for h, k in ((0, 4), (1, NZ - 4)):
        remote(Zs.at[lax.rem(res + 4, RES), h], Zr.at[6, h], q1s_sem, q1r_sem.at[6 + h], dev(dz=k)).start()
    for i, k in enumerate(near):
        remote(Zs.at[lax.rem(res + k, RES)], Zr.at[i], q1s_sem, q1r_sem.at[i], dev(dz=k)).start()
    for h in range(2):
        for i, k in enumerate(near):
            wait(Zb.at[lax.rem(res + 2 * RES - (k if k < RES else k - NZ), RES), h], z2r_sem.at[i, h])
        wait(Zb.at[lax.rem(res + 4, RES), h], z2r_sem.at[6, h])
    mine = rows(x, y)
    for h in range(2):
        for j in range(RES // 2):
            at = 384 * j
            W[x_lo, h, mine, at : at + 128] = Zb[2 * j, h, :, 0:128]
            W[x_lo, h, mine, at + 128 : at + 256] = Zb[2 * j, h, :, 128:256] + Zb[2 * j + 1, h, :, 0:128]
            W[x_lo, h, mine, at + 256 : at + 384] = Zb[2 * j + 1, h, :, 128:256]

    for k in (1, 3, 2):
        for h in range(2):
            here = W.at[x_lo, h, mine]
            remote(here, here, a1s_sem, a1r_sem.at[h, k - 1], over(k, 1 - h)).start()

    def origin(j, k, h):
        return (mod(x - j, NX), mod(y - k, NY)) if h == 0 else (mod(x - k, NX), mod(y - j, NY))

    def part(j, k, h):
        xx, yy = origin(j, k, h)
        return W.at[lax.rem(xx, 2), h, rows(xx, yy)]

    def pass_on(j, h):
        here = part(j, 0, h)
        for k in (1, 3, 2):
            remote(here, here, a2s_sem, a2r_sem.at[h, k - 1, j], over(k, h)).start()

    for h in range(2):
        pass_on(0, h)

    for i in range(6):
        wait(Zr.at[i], q1r_sem.at[i])
    for h in range(2):
        wait(Zr.at[6, h], q1r_sem.at[6 + h])
    total = Zs[res].astype(F32)
    for i in range(7):
        total += Zr[i].astype(F32)
    Zq[...] = total.astype(BF16)

    def out_of(h, k, both):
        return remote(
            Zq.at[h], Zr2.at[k - 1], q2s_sem.at[h, both], q2r_sem.at[k - 1], dev(dz=8 * k, sibling=both == 1)
        )

    for h in range(2):
        for k in (2, 1, 3):

            @pl.when(place[h] == 4 - k)
            def _():
                out_of(h, k, 0).start()
                out_of(h, k, 1).start()

    own = Zq.at[lax.rem(octet, 2)]
    v_copy = remote(own, Zr2.at[3], v_sem.at[0], v_sem.at[1], sib)

    @pl.when(lead)
    def _():
        v_copy.start()
        Zr2[3] = own[...]

    for j in (1, 3, 2):
        for h in range(2):
            wait(part(j, 0, h), a1r_sem.at[h, j - 1])
            pass_on(j, h)

    acc = None
    for xl, h, pieces in (
        (lax.rem(x_lo + 1, 2), 0, [(j, k) for j in (1, 3) for k in (1, 3, 2)]),
        (lax.rem(x_lo + 1, 2), 1, [(j, k) for j in (0, 1, 3, 2) for k in (1, 3)]),
        (x_lo, 0, [(j, k) for j in (0, 2) for k in (1, 3, 2)]),
        (x_lo, 1, [(j, 2) for j in (0, 1, 3, 2)]),
    ):
        for j, k in pieces:
            wait(part(j, k, h), a2r_sem.at[h, k - 1, j])
        term = dot(T[xl, h], W[xl, h], 1, 1)
        acc = term if acc is None else acc + term
    Psum[...] = acc
    p_copy = remote(Psum.at[pl.ds(128, 128)], Pr, p_sem.at[0], p_sem.at[1], sib)
    p_copy.start()

    @pl.when(jnp.logical_not(lead))
    def _():
        v_copy.wait_recv()

    total = Zr2[3].astype(F32)
    for k in (1, 2, 3):
        wait(Zr2.at[k - 1], q2r_sem.at[k - 1])
        total += Zr2[k - 1].astype(F32)
    picked = jnp.where(core == 0, total[0:8], total[8:16])
    wg[...] = jnp.where(odd == 1, picked[:, 64:PAD], picked[:, 0:ROWS])

    p_copy.wait_recv()
    proj[...] = (Psum[0:128] + Pr[...]).astype(BF16)

    p_copy.wait_send()
    cot_copy.wait_send()
    for copy in tok_copy.values():
        copy.wait_send()

    @pl.when(lead)
    def _():
        v_copy.wait_send()

    @pl.when(jnp.logical_not(lead))
    def _():
        a_copy.wait_send()

    wait(Zr, z2s_sem)
    wait(Zr, q1s_sem)
    wait(R1, r1s_sem)
    wait(R1, a2s_sem)
    wait(R2, r2s_sem)
    wait(R2, a1s_sem)
    for h in range(2):

        @pl.when(place[h] != 0)
        def _():
            wait(Zq.at[h], q2s_sem.at[h, 0])
            wait(Zq.at[h], q2s_sem.at[h, 1])

        @pl.when(place[h] == 0)
        def _():
            wait(Zb.at[res, h], z1s_sem.at[h, 1])

        @pl.when(place[h] <= 1)
        def _():
            wait(Zb.at[res, h], z1s_sem.at[h, 0])


def on_device(tokens, weight_codes, block_scales, cotangent):
    vmem = pl.BlockSpec(memory_space=pltpu.VMEM)
    dma = pltpu.SemaphoreType.DMA
    projected, turned = pl.pallas_call(
        kernel,
        out_shape=(
            pltpu.VMEM((128, 128), BF16),
            pltpu.VMEM((8, ROWS), F32),
        ),
        in_specs=[pl.BlockSpec(memory_space=pl.ANY)] * 4,
        out_specs=(vmem, vmem),
        scratch_shapes=[
            pltpu.VMEM((8, ROWS), BF16),
            pltpu.VMEM((8, block_scales.shape[0]), BF16),
            pltpu.VMEM((128, 128), BF16),
            pltpu.VMEM((2, 2, 256, SPAN), BF16),
            pltpu.VMEM((128, 128), BF16),
            pltpu.VMEM((128, 256), BF16),
            pltpu.VMEM((2, 2, 128, SPAN), BF16),
            pltpu.VMEM((2, 2, 128, SPAN), BF16),
            pltpu.VMEM((2, 3, NY * COLS, SPAN), BF16),
            pltpu.VMEM((2, 3, COLS, SPAN), BF16),
            pltpu.VMEM((2, 3, COLS, SPAN), BF16),
            pltpu.VMEM((2, COLS, SPAN), F32),
            pltpu.VMEM((COLS, PAD), BF16),
            pltpu.VMEM((COLS, PAD), BF16),
            pltpu.VMEM((RES, 2, COLS, PAD), BF16),
            pltpu.VMEM((RES, 2, COLS, PAD), BF16),
            pltpu.VMEM((7, 2, COLS, PAD), BF16),
            pltpu.VMEM((2, COLS, PAD), BF16),
            pltpu.VMEM((4, COLS, PAD), BF16),
            pltpu.VMEM((256, 128), F32),
            pltpu.VMEM((128, 128), F32),
            dma((3,)),
            dma((2, 2)),
            dma((2, 2)),
            dma((2, 2)),
            dma((2,)),
            dma((2,)),
            dma((2,)),
            dma((2,)),
            pltpu.SemaphoreType.REGULAR,
            dma((2, 2)),
            dma((2,)),
            dma,
            dma((7, 2)),
            dma,
            dma((2, 3, 4)),
            dma,
            dma((2, 3)),
            dma,
            dma((2, 3)),
            dma,
            dma((2, 3, 4)),
            dma,
            dma((8,)),
            dma((2, 2)),
            dma((3,)),
        ],
        compiler_params=pltpu.CompilerParams(
            collective_id=0, has_side_effects=True, vmem_limit_bytes=60 * 1024 * 1024
        ),
    )(tokens, weight_codes.T, block_scales.T, cotangent)
    return projected, turned.T


def solution(mesh):
    placed = (
        P(("wide", "node"), None),
        P("wide", "node"),
        P(None, "node"),
        P(("wide", "node"), None),
    )
    return jax.shard_map(
        on_device,
        mesh=mesh,
        in_specs=placed,
        out_specs=(P(("wide", "node"), None), P("wide", "node")),
        check_vma=False,
    )
```

```python
import jax
import jax.numpy as jnp
from jax import lax
from jax.experimental import pallas as pl
from jax.experimental.pallas import tpu as pltpu
from jax.sharding import PartitionSpec as P

MESH = pl.DeviceIdType.MESH
BF16 = jnp.bfloat16
F32 = jnp.float32
NX = 4
NY = 4
NZ = 32
RES = 8
ROWS = 192
COLS = 16
SPAN = RES * ROWS
PAD = 256
BLOCK = 128


def mod(a, n):
    return lax.rem(a + n, n)


def dot(a, b, ca, cb):
    return lax.dot_general(a, b, (((ca,), (cb,)), ((), ())), preferred_element_type=F32)


def kernel(
    tok_hbm, codes_hbm, scales_hbm, cot_hbm, proj, wg,
    codes, scales, cot,
    T, C2, cotT, W, G, R1, S1, R2, F0, A, Ar, Zb, Zs, Zr, Zq, Zr2, Psum, Pr,
    in_sem, tl_sem, ts_sem, tr_sem, c_sem, a_sem, v_sem, p_sem,
    n_sem, z1s_sem, z1r_sem, z2s_sem, z2r_sem,
    r1s_sem, r1r_sem, r2s_sem, r2r_sem,
    a1s_sem, a1r_sem, a2s_sem, a2r_sem,
    q1s_sem, q1r_sem, q2s_sem, q2r_sem,
):
    wide, node = lax.axis_index("wide"), lax.axis_index("node")
    x_lo, z = wide // NZ, lax.rem(wide, NZ)
    x_hi, y, core = node // (2 * NY), lax.rem(node // 2, NY), lax.rem(node, 2)
    x = 2 * x_hi + x_lo
    res, octet = lax.rem(z, RES), z // RES
    odd = lax.rem(z, 2)
    lead = core == z // 16

    def dev(dx=0, dy=0, dz=0, sibling=False):
        xx, yy, zz = lax.rem(x + dx, NX), lax.rem(y + dy, NY), lax.rem(z + dz, NZ)
        cc = 1 - core if sibling else core
        return (lax.rem(xx, 2) * NZ + zz, (xx // 2) * (2 * NY) + yy * 2 + cc)

    def rows(xx, yy):
        return pl.ds(pl.multiple_of(COLS * ((xx // 2) * NY + yy), COLS), COLS)

    def remote(src, dst, send, recv, to):
        return pltpu.make_async_remote_copy(
            src_ref=src, dst_ref=dst, send_sem=send, recv_sem=recv, device_id=to, device_id_type=MESH
        )

    def wait(ref, sem):
        pltpu.make_async_copy(ref, ref, sem).wait()

    near = (3, NZ - 3, 2, NZ - 2, 1, NZ - 1)
    partners = [dev(sibling=True)]
    partners += [dev(dx=k) for k in (1, 2, 3)] + [dev(dy=k) for k in (1, 2, 3)]
    partners += [dev(dz=k) for k in near + (4, NZ - 4)]

    barrier = pltpu.get_barrier_semaphore()
    for to in partners:
        pl.semaphore_signal(barrier, inc=1, device_id=to, device_id_type=MESH)

    loads = [
        pltpu.make_async_copy(src, dst, in_sem.at[i])
        for i, (src, dst) in enumerate(((codes_hbm, codes), (scales_hbm, scales), (cot_hbm, cot)))
    ]
    for load in loads:
        load.start()

    def columns(xl, half, h):
        return pl.ds(pl.multiple_of(xl * NZ * ROWS + half * 2 * SPAN + h * SPAN, SPAN), SPAN)

    chunks = [(lax.rem(x_lo + 1 + a, 2), a, h) for a in range(2) for h in range(2)]
    for xl, a, h in chunks:
        pltpu.make_async_copy(
            tok_hbm.at[:, columns(xl, core, h)], T.at[xl, h, pl.ds(0, 128)], tl_sem.at[a, h]
        ).start()

    loads[0].wait()
    loads[1].wait()
    nb = scales.shape[1]
    block_of = (lax.broadcasted_iota(jnp.int32, (ROWS, nb), 0) + wide * ROWS) // BLOCK
    pick = (block_of == lax.broadcasted_iota(jnp.int32, (ROWS, nb), 1)).astype(BF16)
    factor = dot(scales[...], pick, 1, 1)
    weight = (codes[...].astype(F32) * factor).astype(BF16).astype(F32)
    blank = jnp.zeros((8, PAD - ROWS), F32)
    weight = jnp.where(odd == 1, jnp.concatenate([blank, weight], 1), jnp.concatenate([weight, blank], 1))
    blank = jnp.zeros((8, PAD), F32)
    A[...] = jnp.where(
        core == 0, jnp.concatenate([weight, blank], 0), jnp.concatenate([blank, weight], 0)
    ).astype(BF16)
    eye = (lax.broadcasted_iota(jnp.int32, (128, 128), 0) == lax.broadcasted_iota(jnp.int32, (128, 128), 1)).astype(BF16)

    pl.semaphore_wait(barrier, len(partners))
    for k in (4, NZ - 4):
        pl.semaphore_signal(n_sem, inc=1, device_id=dev(dz=k), device_id_type=MESH)

    sib = dev(sibling=True)
    a_copy = remote(A, Ar, a_sem.at[0], a_sem.at[1], sib)

    @pl.when(jnp.logical_not(lead))
    def _():
        a_copy.start()

    cot_copy = remote(cot_hbm, C2, c_sem.at[0], c_sem.at[1], sib)
    cot_copy.start()
    tok_copy = {}
    for xl, a, h in chunks:
        tok_copy[a, h] = remote(
            tok_hbm.at[:, columns(xl, 1 - core, h)],
            T.at[xl, h, pl.ds(128, 128)],
            ts_sem.at[a, h],
            tr_sem.at[a, h],
            sib,
        )
        tok_copy[a, h].start()

    loads[2].wait()
    cotT[:, pl.ds(0, 128)] = dot(eye, cot[...], 1, 1).astype(BF16)
    cot_copy.wait_recv()
    cotT[:, pl.ds(128, 128)] = dot(eye, C2[...], 1, 1).astype(BF16)

    def grad(xl, a, h):
        wait(T.at[xl, h, pl.ds(0, 128)], tl_sem.at[a, h])
        tok_copy[a, h].wait_recv()

        def tile(i, carry):
            at = pl.ds(pl.multiple_of(i * 512, 512), 512)
            G[xl, h, :, at] = dot(cotT[...], T[xl, h, :, at], 1, 0).astype(BF16)
            return carry

        lax.fori_loop(0, SPAN // 512, tile, 0)

    def piece(j, k, h):
        return (lax.rem(x + j, NX), lax.rem(y + k, NY)) if h == 0 else (lax.rem(x + k, NX), lax.rem(y + j, NY))

    def over(k, h):
        return dev(dy=k) if h == 0 else dev(dx=k)

    def send_grad(a, h):
        if h == 0:
            pairs = [(j, k) for j in ((1, 3), (2, 0))[a] for k in (2, 1, 3)]
        else:
            pairs = [(0, k) for k in ((1, 3), (2,))[a]]
        for j, k in pairs:
            xx, yy = piece(j, k, h)
            if h == 0:
                here, there = rows(xx, yy), pl.ds(COLS * j, COLS)
            else:
                here, there = pl.ds(pl.multiple_of(NY * COLS * (xx // 2), NY * COLS), NY * COLS), pl.ds(0, NY * COLS)
            remote(
                G.at[lax.rem(xx, 2), h, here], R1.at[h, k - 1, there], r1s_sem, r1r_sem.at[h, k - 1, j], over(k, h)
            ).start()

    grad(*chunks[0])
    send_grad(*chunks[0][1:])

    pl.semaphore_wait(n_sem, 2)

    def onward(h, i, k):
        here = Zb.at[res, h]
        return remote(here, here, z1s_sem.at[h, i], z1r_sem.at[h], dev(dz=k))

    place = [lax.rem(octet - 2 * core - h + 4, 4) for h in range(2)]

    @pl.when(lead)
    def _():
        wait(Ar, a_sem.at[1])
        for h in range(2):

            @pl.when(place[h] == 0)
            def _():
                Zb[res, h] = A[...] + Ar[...]
                onward(h, 0, 8).start()
                onward(h, 1, 24).start()

    for xl, a, h in chunks[1:]:
        grad(xl, a, h)
        send_grad(a, h)

    for h in range(2):

        @pl.when(place[h] == 1)
        def _():
            wait(Zb.at[res, h], z1r_sem.at[h])
            onward(h, 0, 8).start()

    first = jnp.where((place[0] == 0) | (place[0] == 3), 0, 1)

    def place_of(h):
        return jnp.where(h == 0, place[0], place[1])

    def spread(h):
        here = Zb.at[res, h]
        remote(here, here, z2s_sem, z2r_sem.at[6, h], dev(dz=jnp.where(h == 0, 4, NZ - 4))).start()
        for i, k in enumerate(near):
            remote(here, here, z2s_sem, z2r_sem.at[i, h], dev(dz=k)).start()

    @pl.when(place_of(first) == 3)
    def _():
        wait(Zb.at[res, first], z1r_sem.at[first])

    spread(first)

    @pl.when(place_of(1 - first) >= 2)
    def _():
        wait(Zb.at[res, 1 - first], z1r_sem.at[1 - first])

    spread(1 - first)

    for h in range(2):
        for j in (1, 3, 2, 0):
            xx, yy = piece(j, 0, h)
            total = G[lax.rem(xx, 2), h, rows(xx, yy)].astype(F32)
            there = pl.ds(COLS * j if h == 0 else pl.multiple_of(COLS * yy, COLS), COLS)
            for k in (1, 3, 2):
                if h == 0:
                    wait(R1.at[h, k - 1, there], r1r_sem.at[h, k - 1, j])
                elif j == 1:
                    wait(R1.at[h, k - 1], r1r_sem.at[h, k - 1, 0])
                total += R1[h, k - 1, there].astype(F32)
            if j == 0:
                F0[h] = total
            else:
                S1[h, j - 1] = total.astype(BF16)
                remote(S1.at[h, j - 1], R2.at[h, j - 1], r2s_sem, r2r_sem.at[h, j - 1], over(j, 1 - h)).start()

    for h in range(2):
        total = F0[h]
        for j in (1, 3, 2):
            wait(R2.at[h, j - 1], r2r_sem.at[h, j - 1])
            total += R2[h, j - 1].astype(F32)
        total = total.astype(BF16)
        for j in range(RES // 2):
            Zs[2 * j, h] = total[:, 384 * j : 384 * j + 256]
            Zs[2 * j + 1, h] = total[:, 384 * j + 128 : 384 * j + 384]

    for h, k in ((0, 4), (1, NZ - 4)):
        remote(Zs.at[lax.rem(res + 4, RES), h], Zr.at[6, h], q1s_sem, q1r_sem.at[6 + h], dev(dz=k)).start()
    for i, k in enumerate(near):
        remote(Zs.at[lax.rem(res + k, RES)], Zr.at[i], q1s_sem, q1r_sem.at[i], dev(dz=k)).start()
    for h in range(2):
        for i, k in enumerate(near):
            wait(Zb.at[lax.rem(res + 2 * RES - (k if k < RES else k - NZ), RES), h], z2r_sem.at[i, h])
        wait(Zb.at[lax.rem(res + 4, RES), h], z2r_sem.at[6, h])
    mine = rows(x, y)
    for h in range(2):
        for j in range(RES // 2):
            at = 384 * j
            W[x_lo, h, mine, at : at + 128] = Zb[2 * j, h, :, 0:128]
            W[x_lo, h, mine, at + 128 : at + 256] = Zb[2 * j, h, :, 128:256] + Zb[2 * j + 1, h, :, 0:128]
            W[x_lo, h, mine, at + 256 : at + 384] = Zb[2 * j + 1, h, :, 128:256]

    for k in (1, 3, 2):
        for h in range(2):
            here = W.at[x_lo, h, mine]
            remote(here, here, a1s_sem, a1r_sem.at[h, k - 1], over(k, 1 - h)).start()

    def origin(j, k, h):
        return (mod(x - j, NX), mod(y - k, NY)) if h == 0 else (mod(x - k, NX), mod(y - j, NY))

    def part(j, k, h):
        xx, yy = origin(j, k, h)
        return W.at[lax.rem(xx, 2), h, rows(xx, yy)]

    def pass_on(j, h):
        here = part(j, 0, h)
        for k in (1, 3, 2):
            remote(here, here, a2s_sem, a2r_sem.at[h, k - 1, j], over(k, h)).start()

    for h in range(2):
        pass_on(0, h)

    for i in range(6):
        wait(Zr.at[i], q1r_sem.at[i])
    for h in range(2):
        wait(Zr.at[6, h], q1r_sem.at[6 + h])
    total = Zs[res].astype(F32)
    for i in range(7):
        total += Zr[i].astype(F32)
    for h in range(2):
        for c in range(2):
            half = total[h, 8 * c : 8 * c + 8]
            Zq[h, c] = jnp.concatenate([half[:, 0:128], half[:, 128:256]], 0).astype(BF16)

    def out_of(h, k, both):
        return remote(
            Zq.at[h, 1 - core if both else core], Zr2.at[k - 1], q2s_sem.at[h, both], q2r_sem.at[k - 1], dev(dz=8 * k, sibling=both == 1)
        )

    for h in range(2):
        for k in (2, 1, 3):

            @pl.when(place[h] == 4 - k)
            def _():
                out_of(h, k, 0).start()
                out_of(h, k, 1).start()

    own = lax.rem(octet, 2)
    v_copy = remote(Zq.at[own, 1 - core], Zr2.at[3], v_sem.at[0], v_sem.at[1], sib)

    @pl.when(lead)
    def _():
        v_copy.start()
        Zr2[3] = Zq[own, core]

    for j in (1, 3, 2):
        for h in range(2):
            wait(part(j, 0, h), a1r_sem.at[h, j - 1])
            pass_on(j, h)

    acc = None
    for xl, h, pieces in (
        (lax.rem(x_lo + 1, 2), 0, [(j, k) for j in (1, 3) for k in (1, 3, 2)]),
        (lax.rem(x_lo + 1, 2), 1, [(j, k) for j in (0, 1, 3, 2) for k in (1, 3)]),
        (x_lo, 0, [(j, k) for j in (0, 2) for k in (1, 3, 2)]),
        (x_lo, 1, [(j, 2) for j in (0, 1, 3, 2)]),
    ):
        for j, k in pieces:
            wait(part(j, k, h), a2r_sem.at[h, k - 1, j])
        if acc is not None and len(pieces) == 4:
            break
        term = dot(T[xl, h], W[xl, h], 1, 1)
        acc = term if acc is None else acc + term
    Psum[128:256] = acc[128:256] + dot(T[xl, h, 128:256], W[xl, h], 1, 1)
    p_copy = remote(Psum.at[pl.ds(128, 128)], Pr, p_sem.at[0], p_sem.at[1], sib)
    p_copy.start()
    Psum[0:128] = acc[0:128] + dot(T[xl, h, 0:128], W[xl, h], 1, 1)

    @pl.when(jnp.logical_not(lead))
    def _():
        v_copy.wait_recv()

    total = Zr2[3].astype(F32)
    for k in (1, 2, 3):
        wait(Zr2.at[k - 1], q2r_sem.at[k - 1])
        total += Zr2[k - 1].astype(F32)
    total = jnp.concatenate([total[0:8], total[8:16]], 1)
    wg[...] = jnp.where(odd == 1, total[:, 64:PAD], total[:, 0:ROWS])

    p_copy.wait_recv()
    proj[...] = (Psum[0:128] + Pr[...]).astype(BF16)

    p_copy.wait_send()
    cot_copy.wait_send()
    for copy in tok_copy.values():
        copy.wait_send()

    @pl.when(lead)
    def _():
        v_copy.wait_send()

    @pl.when(jnp.logical_not(lead))
    def _():
        a_copy.wait_send()

    wait(Zr, z2s_sem)
    wait(Zr, q1s_sem)
    wait(R1, r1s_sem)
    wait(R1, a2s_sem)
    wait(R2, r2s_sem)
    wait(R2, a1s_sem)
    for h in range(2):

        @pl.when(place[h] != 0)
        def _():
            wait(Zq.at[h, 0], q2s_sem.at[h, 0])
            wait(Zq.at[h, 1], q2s_sem.at[h, 1])

        @pl.when(place[h] == 0)
        def _():
            wait(Zb.at[res, h], z1s_sem.at[h, 1])

        @pl.when(place[h] <= 1)
        def _():
            wait(Zb.at[res, h], z1s_sem.at[h, 0])


def on_device(tokens, weight_codes, block_scales, cotangent):
    vmem = pl.BlockSpec(memory_space=pltpu.VMEM)
    dma = pltpu.SemaphoreType.DMA
    projected, turned = pl.pallas_call(
        kernel,
        out_shape=(
            pltpu.VMEM((128, 128), BF16),
            pltpu.VMEM((8, ROWS), F32),
        ),
        in_specs=[pl.BlockSpec(memory_space=pl.ANY)] * 4,
        out_specs=(vmem, vmem),
        scratch_shapes=[
            pltpu.VMEM((8, ROWS), BF16),
            pltpu.VMEM((8, block_scales.shape[0]), BF16),
            pltpu.VMEM((128, 128), BF16),
            pltpu.VMEM((2, 2, 256, SPAN), BF16),
            pltpu.VMEM((128, 128), BF16),
            pltpu.VMEM((128, 256), BF16),
            pltpu.VMEM((2, 2, 128, SPAN), BF16),
            pltpu.VMEM((2, 2, 128, SPAN), BF16),
            pltpu.VMEM((2, 3, NY * COLS, SPAN), BF16),
            pltpu.VMEM((2, 3, COLS, SPAN), BF16),
            pltpu.VMEM((2, 3, COLS, SPAN), BF16),
            pltpu.VMEM((2, COLS, SPAN), F32),
            pltpu.VMEM((COLS, PAD), BF16),
            pltpu.VMEM((COLS, PAD), BF16),
            pltpu.VMEM((RES, 2, COLS, PAD), BF16),
            pltpu.VMEM((RES, 2, COLS, PAD), BF16),
            pltpu.VMEM((7, 2, COLS, PAD), BF16),
            pltpu.VMEM((2, 2, COLS, 128), BF16),
            pltpu.VMEM((4, COLS, 128), BF16),
            pltpu.VMEM((256, 128), F32),
            pltpu.VMEM((128, 128), F32),
            dma((3,)),
            dma((2, 2)),
            dma((2, 2)),
            dma((2, 2)),
            dma((2,)),
            dma((2,)),
            dma((2,)),
            dma((2,)),
            pltpu.SemaphoreType.REGULAR,
            dma((2, 2)),
            dma((2,)),
            dma,
            dma((7, 2)),
            dma,
            dma((2, 3, 4)),
            dma,
            dma((2, 3)),
            dma,
            dma((2, 3)),
            dma,
            dma((2, 3, 4)),
            dma,
            dma((8,)),
            dma((2, 2)),
            dma((3,)),
        ],
        compiler_params=pltpu.CompilerParams(
            collective_id=0, has_side_effects=True, vmem_limit_bytes=60 * 1024 * 1024
        ),
    )(tokens, weight_codes.T, block_scales.T, cotangent)
    return projected, turned.T


def solution(mesh):
    placed = (
        P(("wide", "node"), None),
        P("wide", "node"),
        P(None, "node"),
        P(("wide", "node"), None),
    )
    return jax.shard_map(
        on_device,
        mesh=mesh,
        in_specs=placed,
        out_specs=(P(("wide", "node"), None), P("wide", "node")),
        check_vma=False,
    )
```
